512 devices in a mesh: neuron: 32 (over z_lo, x, core), pos: 4 (over y), trial: 4 (over z_hi).
Axes of the slice: x: 4, y: 4, z: 16 (z_hi: 4, z_lo: 4; z = z_hi * 4 + z_lo), core: 2. Of those that a mesh axis runs over, the one named last changes fastest.
Arguments:
- counts: int32 [64, 256, 16384], P('trial', 'pos', 'neuron'), may hold values from 0 to 7
- neuron_factors: float32 [16, 16384], P(None, 'neuron'), may hold values from 0.2 to 1
- pos_factors: float32 [16, 256], P(None, 'pos'), may hold values from 0.2 to 1
- trial_factors: float32 [16, 64], P(None, 'trial'), may hold values from 0.2 to 1
Outputs:
- grad_neuron: float32 [16, 16384], replicated
- grad_pos: float32 [16, 256], replicated
- grad_trial: float32 [16, 64], replicated
The draws below stay inside these ranges and needn't reach their ends.
All inputs are finite; a program needn't handle non-finite values.
Results may differ from the reference program's by a relative error of at most 0.0001.
Values sent between devices are 32-bit elements; how exact they have to be, the bound alone decides.
A program may use at most 64 MiB of HBM per device.

```python
import math
import jax
import jax.numpy as jnp
from jax import lax

RANK = 16
NEURONS = 16384
POS = 256
TRIALS = 64


def plant(result, own_key, smallest, top_value):
    place = [jax.random.randint(jax.random.fold_in(own_key, axis), (), 0, length) for axis, length in enumerate(result.shape)]
    main_axis = result.shape.index(max(result.shape))
    next_to = place[:main_axis] + [(place[main_axis] + 1) % result.shape[main_axis]] + place[main_axis + 1:]
    return result.at[tuple(place)].set(smallest).at[tuple(next_to)].set(top_value)


def shard_levels(key, dims, shards, low, high):
    gain, own = 1.0, jax.random.fold_in(key, 6)
    for axis_at, blocks in shards:
        heights = jnp.exp(jax.random.uniform(jax.random.fold_in(own, axis_at), (blocks,), jnp.float32, low / len(shards), high / len(shards)))
        gain = gain * jnp.repeat(heights, dims[axis_at] // blocks).reshape([-1 if axis == axis_at else 1 for axis in range(len(dims))])
    return gain


def setup_inputs(seed: int = 0) -> dict:
    seeds = jax.random.split(jax.random.key(seed), 5)
    return {
        "counts": plant(jax.random.randint(seeds[0], (TRIALS, POS, NEURONS), 0, 8), jax.random.fold_in(seeds[0], 1), 0, 7).astype(jnp.int32),
        "neuron_factors": jnp.clip(jnp.exp(math.log(1.0) - 1.609438 * jax.random.uniform(seeds[1], (RANK, NEURONS), jnp.float32) ** shard_levels(seeds[1], (RANK, NEURONS), ((1, 32),), -0.2, 0.2)), 0.2, 1.0),
        "pos_factors": jnp.clip(jnp.exp(math.log(1.0) - 1.609438 * jax.random.uniform(seeds[2], (RANK, POS), jnp.float32) ** shard_levels(seeds[2], (RANK, POS), ((1, 4),), -0.2, 0.2)), 0.2, 1.0),
        "trial_factors": jnp.clip(jnp.exp(math.log(1.0) - 1.609438 * jax.random.uniform(seeds[3], (RANK, TRIALS), jnp.float32) ** shard_levels(seeds[3], (RANK, TRIALS), ((1, 4),), -0.2, 0.2)), 0.2, 1.0),
    }


def reference(counts, neuron_factors, pos_factors, trial_factors):
    highest = lax.Precision.HIGHEST

    def one_trial(carry, inputs):
        grad_a, grad_b = carry
        block, column = inputs
        weights = pos_factors * column[:, None]
        model = jnp.dot(weights.T, neuron_factors, precision=highest)
        ratio = 1.0 - block.astype(jnp.float32) / model
        grad_a = grad_a + jnp.dot(weights, ratio, precision=highest)
        projected = jnp.dot(ratio, neuron_factors.T, precision=highest)
        grad_b = grad_b + projected.T * column[:, None]
        grad_c = jnp.sum(projected.T * pos_factors, axis=1)
        return (grad_a, grad_b), grad_c

    start = (jnp.zeros(neuron_factors.shape, jnp.float32), jnp.zeros(pos_factors.shape, jnp.float32))
    (grad_a, grad_b), grad_c = lax.scan(one_trial, start, (counts, trial_factors.T))
    grad_neuron = grad_a / (POS * TRIALS)
    grad_pos = grad_b / (NEURONS * TRIALS)
    grad_trial = grad_c.T / (NEURONS * POS)
    return grad_neuron, grad_pos, grad_trial
```

```python
import jax
import jax.numpy as jnp
from jax import lax
from jax.experimental import pallas as pl
from jax.experimental.pallas import tpu as pltpu
from jax.sharding import PartitionSpec as P

MESH = pl.DeviceIdType.MESH
RING = (0, 1, -1, 2)
LANES = 128


def split(value):
    high = value.astype(jnp.bfloat16).astype(jnp.float32)
    return high, value - high


def kernel(
    counts_hbm, nf_ref, pf_ref, tf_ref, gn_ref, gp_ref, gt_ref,
    counts, stage, proj, part_a, sum_a, part_v, sum_v, mean_v, far_v, final,
    a1, a2, v1, v2, v3, other,
    counts_sem, a1_s, a1_r, a2_s, a2_r, a3_s, a3_r, a4_s, a4_r, v1_s, v1_r, v2_s, v2_r, v3_s, v3_r, v4_s, v4_r,
):
    ranks, i_dev = nf_ref.shape
    j_dev, k_dev = pf_ref.shape[1], tf_ref.shape[1]
    neurons = i_dev * lax.axis_size("neuron")
    positions = j_dev * lax.axis_size("pos")
    trials = k_dev * lax.axis_size("trial")
    chunks = counts.shape[0]
    k_chunk = k_dev // chunks
    rows = k_chunk * j_dev

    loads = []
    for chunk in range(chunks):
        load = pltpu.make_async_copy(
            counts_hbm.at[pl.ds(chunk * k_chunk, k_chunk)], counts.at[chunk], counts_sem.at[chunk]
        )
        load.start()
        loads.append(load)

    me, y, z_hi = lax.axis_index("neuron"), lax.axis_index("pos"), lax.axis_index("trial")
    core, x, z_lo = lax.rem(me, 2), lax.rem(me // 2, 4), me // 8
    z = z_hi * 4 + z_lo
    sign = 1 - 2 * core
    steps_z = (0, 1, -1, 2 * sign)
    xs = [lax.rem(x + 4 + d, 4) for d in RING]
    xs_back = [lax.rem(x + 4 - d, 4) for d in RING]
    ys = [lax.rem(y + 4 + d, 4) for d in RING]
    ys_back = [lax.rem(y + 4 - d, 4) for d in RING]
    zs = [lax.rem(z + 16 + d, 16) for d in steps_z]
    zs_back = [lax.rem(z + 16 - d, 16) for d in steps_z]
    his = [lax.rem(z_hi + 4 + d, 4) for d in RING]
    his_back = [lax.rem(z_hi + 4 - d, 4) for d in RING]

    def at(x_, y_, z_, core_):
        return {"neuron": (lax.rem(z_, 4) * 4 + x_) * 2 + core_, "pos": y_, "trial": z_ // 4}

    def column(x_, z_):
        return (lax.rem(z_, 4) * 4 + x_) * 2 * i_dev

    cube = [(a, b, c) for c in (3, 1, 2, 0) for b in (3, 1, 2, 0) for a in (3, 1, 2, 0) if a or b or c]

    barrier = pltpu.get_barrier_semaphore()
    greeted = 0
    for a, b, c in cube:
        pl.semaphore_signal(barrier, inc=1, device_id=at(xs_back[a], ys_back[b], zs_back[c], core), device_id_type=MESH)
        greeted += 1
    for a in range(4):
        pl.semaphore_signal(barrier, inc=1, device_id=at(xs_back[a], y, z, 1 - core), device_id_type=MESH)
        greeted += 1
    for h in (1, 2, 3):
        pl.semaphore_signal(barrier, inc=1, device_id={"neuron": me, "pos": y, "trial": his_back[h]}, device_id_type=MESH)
        greeted += 1

    nf, pf, tf = nf_ref[...], pf_ref[...], tf_ref[...]
    stage[...] = jnp.zeros_like(stage)
    for group in range(4):
        stage[pl.ds(group * ranks, ranks), pl.ds(0, j_dev)] = pf
        stage[pl.ds(group * ranks, ranks), pl.ds(j_dev, k_dev)] = tf
    turned = stage[...].T
    pf_t, tf_t = turned[:j_dev], turned[j_dev : j_dev + k_dev]
    lane = lax.broadcasted_iota(jnp.int32, (j_dev, LANES), 1)
    use_high = lax.rem(lane // ranks, 2) == 0
    nf_high, nf_low = split(nf)
    blank = jnp.zeros((LANES - 4 * ranks, i_dev), jnp.float32)
    nf_model = jnp.concatenate([nf_high, nf_high, nf_low, nf_low, blank], axis=0).astype(jnp.bfloat16)
    blank = jnp.zeros((LANES - 2 * ranks, i_dev), jnp.float32)
    nf_proj = jnp.concatenate([nf_high, nf_low, blank], axis=0).astype(jnp.bfloat16)
    pf_pair = jnp.concatenate([pf, pf], axis=1)
    left = lax.broadcasted_iota(jnp.int32, (ranks, LANES), 1) < j_dev

    half = 256
    acc = [jnp.zeros((2 * ranks, half), jnp.float32) for _ in range(i_dev // half)]
    for chunk in range(chunks):
        k0 = chunk * k_chunk
        weights_t = []
        for k in range(k0, k0 + k_chunk):
            high, low = split(pf_t * tf_t[k : k + 1])
            weights_t.append(jnp.where(use_high, high, low))
        weights_t = jnp.concatenate(weights_t, axis=0).astype(jnp.bfloat16)
        highs, lows = [], []
        for k in range(k0, k0 + k_chunk, 2):
            high, low = split(pf_pair * jnp.where(left, tf[:, k : k + 1], tf[:, k + 1 : k + 2]))
            highs.append(high)
            lows.append(low)
        weights = jnp.concatenate(
            [jnp.concatenate(highs, axis=1), jnp.concatenate(lows, axis=1)], axis=0
        ).astype(jnp.bfloat16)
        loads[chunk].wait()
        projected = jnp.zeros((rows, LANES), jnp.float32)
        for part in range(i_dev // half):
            cols = slice(part * half, (part + 1) * half)
            model = jnp.dot(weights_t, nf_model[:, cols], preferred_element_type=jnp.float32)
            guess = pl.reciprocal(model, approx=True)
            inverse = guess * (2.0 - model * guess)
            spikes = counts[chunk, :, :, cols].reshape(rows, half).astype(jnp.float32)
            ratio = 1.0 - spikes * inverse
            high = ratio.astype(jnp.bfloat16)
            low = (ratio - high.astype(jnp.float32)).astype(jnp.bfloat16)
            for piece in (high, low):
                acc[part] = acc[part] + jnp.dot(weights, piece, preferred_element_type=jnp.float32)
                projected = projected + lax.dot_general(
                    piece, nf_proj[:, cols], (((1,), (1,)), ((), ())), preferred_element_type=jnp.float32
                )
        proj[pl.ds(k0 * j_dev, rows), :] = projected
    for part in range(i_dev // half):
        part_a[:, pl.ds(part * half, half)] = (acc[part][:ranks] + acc[part][ranks:]) / (positions * trials)

    pl.semaphore_wait(barrier, greeted)

    def send(src, dst, send_sem, recv_sem, device):
        copy = pltpu.make_async_remote_copy(
            src_ref=src, dst_ref=dst, send_sem=send_sem, recv_sem=recv_sem, device_id=device, device_id_type=MESH
        )
        copy.start()
        return copy

    quarter = i_dev // 4

    def quarter_of(index):
        return part_a.at[:, pl.ds(pl.multiple_of(index * quarter, quarter), quarter)]

    first_a = [
        send(quarter_of(ys[d]), a1.at[d - 1], a1_s.at[d - 1], a1_r.at[d - 1], {"neuron": me, "pos": ys[d], "trial": z_hi})
        for d in (3, 1, 2)
    ]

    grad_b = jnp.zeros((j_dev, LANES), jnp.float32)
    grad_c = []
    for k in range(k_dev):
        block = proj[pl.ds(k * j_dev, j_dev), :]
        grad_b = grad_b + block * tf_t[k : k + 1]
        grad_c.append(jnp.sum(block * pf_t, axis=0, keepdims=True))
    stage[pl.ds(0, j_dev), :] = grad_b / (neurons * trials)
    stage[pl.ds(j_dev, LANES - j_dev), :] = jnp.zeros((LANES - j_dev, LANES), jnp.float32)
    stage[pl.ds(pl.multiple_of(j_dev + z_hi * k_dev, k_dev), k_dev), :] = jnp.concatenate(grad_c, axis=0) / (
        neurons * positions
    )
    turned = stage[...].T
    part_v[...] = (turned[:ranks] + turned[ranks : 2 * ranks]).reshape(part_v.shape)
    first_v = []
    for a in range(4):
        for c in range(2):
            if a or c:
                other_core = core if c == 0 else 1 - core
                slot = a * 2 + c - 1
                first_v.append(
                    send(part_v.at[other_core], v1.at[slot], v1_s.at[slot], v1_r.at[slot], at(xs[a], y, z, other_core))
                )

    for copy in first_a:
        copy.wait_recv()
    sum_a[...] = (a1[0] + a1[1]) + (a1[2] + quarter_of(y)[...])
    second_a = [
        send(sum_a, a2.at[h - 1], a2_s.at[h - 1], a2_r.at[h - 1], {"neuron": me, "pos": y, "trial": his[h]})
        for h in (3, 1, 2)
    ]
    for copy in first_v:
        copy.wait_recv()
    total = part_v[core]
    for slot in range(7):
        total = total + v1[slot]
    sum_v[...] = total
    second_v = [
        send(sum_v, v2.at[h - 1], v2_s.at[h - 1], v2_r.at[h - 1], {"neuron": me, "pos": y, "trial": his[h]})
        for h in (3, 1, 2)
    ]

    for copy in second_a:
        copy.wait_recv()
    mine = gn_ref.at[:, pl.ds(pl.multiple_of(me * i_dev + y * quarter, quarter), quarter)]
    mine[...] = (a2[0] + a2[1]) + (a2[2] + sum_a[...])
    for a, b, c in cube:
        send(mine, mine, a3_s, a3_r.at[c * 4 + a], at(xs[a], ys[b], zs[c], core))
    for copy in second_v:
        copy.wait_recv()
    mean_v[...] = (v2[0] + v2[1]) + (v2[2] + sum_v[...])
    third_v = []
    for b in (3, 1, 2, 0):
        for c in (3, 1, 2, 0):
            if b or c:
                slot = c * 4 + b
                third_v.append(
                    send(mean_v, v3.at[slot], v3_s.at[slot], v3_r.at[slot], at(x, ys[b], zs[c], core))
                )
    v3[0] = mean_v[...]

    partner = {"neuron": me + sign, "pos": y, "trial": z_hi}

    def block_of(start):
        return gn_ref.at[:, pl.ds(pl.multiple_of(start, i_dev), i_dev)]

    fourth = []
    for c in (0, 1, 2, 3):
        for a in (0, 1, 2, 3):
            slot = c * 4 + a
            block = block_of(column(xs_back[a], zs_back[c]) + core * i_dev)
            if slot == 0:
                landed = gn_ref.at[:, pl.ds(0, 3 * quarter)]
            else:
                landed = block
            pltpu.make_async_copy(landed, landed, a3_r.at[slot]).wait()
            fourth.append(send(block, block, a4_s.at[slot], a4_r.at[slot], partner))
    for copy in third_v:
        copy.wait_recv()
    all_c = jnp.zeros((8, LANES), jnp.float32)
    for b in range(4):
        over_z = (v3[b] + v3[4 + b]) + (v3[8 + b] + v3[12 + b])
        all_c = all_c + over_z
        far_v[ys_back[b]] = over_z
    final[4] = all_c
    for b in range(4):
        final[b] = far_v[b]
    swap = send(final, other, v4_s, v4_r, partner)

    def write(ref, row):
        for b in range(4):
            gp_ref[pl.ds(row, 8), pl.ds(b * j_dev, j_dev)] = ref[b][:, :j_dev]
        gt_ref[pl.ds(row, 8), :] = ref[4][:, j_dev:]

    write(final, pl.multiple_of(core * 8, 8))
    swap.wait_recv()
    write(other, pl.multiple_of((1 - core) * 8, 8))
    for copy in fourth:
        copy.wait_recv()

    for copy in first_a + first_v + second_a + second_v + third_v + fourth + [swap]:
        copy.wait_send()
    sent = gn_ref.at[:, pl.ds(0, len(cube) * quarter)]
    pltpu.make_async_copy(sent, sent, a3_s).wait()


def body(counts, neuron_factors, pos_factors, trial_factors):
    k_dev, j_dev, i_dev = counts.shape
    ranks = neuron_factors.shape[0]
    chunks = 4
    vmem = pl.BlockSpec(memory_space=pltpu.VMEM)
    f32 = jnp.float32
    dma = pltpu.SemaphoreType.DMA
    return pl.pallas_call(
        kernel,
        name="gradients",
        out_shape=(
            jax.ShapeDtypeStruct((ranks, i_dev * lax.axis_size("neuron")), f32),
            jax.ShapeDtypeStruct((ranks, j_dev * lax.axis_size("pos")), f32),
            jax.ShapeDtypeStruct((ranks, k_dev * lax.axis_size("trial")), f32),
        ),
        in_specs=[pl.BlockSpec(memory_space=pl.ANY), vmem, vmem, vmem],
        out_specs=(vmem, vmem, vmem),
        scratch_shapes=[
            pltpu.VMEM((chunks, k_dev // chunks, j_dev, i_dev), jnp.int32),
            pltpu.VMEM((LANES, LANES), f32),
            pltpu.VMEM((k_dev * j_dev, LANES), f32),
            pltpu.VMEM((ranks, i_dev), f32),
            pltpu.VMEM((ranks, LANES), f32),
            pltpu.VMEM((2, 8, LANES), f32),
            pltpu.VMEM((8, LANES), f32),
            pltpu.VMEM((8, LANES), f32),
            pltpu.VMEM((4, 8, LANES), f32),
            pltpu.VMEM((5, 8, LANES), f32),
            pltpu.VMEM((3, ranks, LANES), f32),
            pltpu.VMEM((3, ranks, LANES), f32),
            pltpu.VMEM((7, 8, LANES), f32),
            pltpu.VMEM((3, 8, LANES), f32),
            pltpu.VMEM((16, 8, LANES), f32),
            pltpu.VMEM((5, 8, LANES), f32),
            dma((chunks,)),
            dma((3,)), dma((3,)), dma((3,)), dma((3,)),
            dma, dma((16,)), dma((16,)), dma((16,)),
            dma((7,)), dma((7,)), dma((3,)), dma((3,)),
            dma((16,)), dma((16,)), dma, dma,
        ],
        compiler_params=pltpu.CompilerParams(
            collective_id=0, has_side_effects=True, vmem_limit_bytes=32 << 20
        ),
    )(counts, neuron_factors, pos_factors, trial_factors)


def solution(mesh):
    placed = (P("trial", "pos", "neuron"), P(None, "neuron"), P(None, "pos"), P(None, "trial"))
    return jax.shard_map(
        body, mesh=mesh, in_specs=placed, out_specs=(P(), P(), P()), check_vma=False
    )
```

```python
import jax
import jax.numpy as jnp
from jax import lax
from jax.experimental import pallas as pl
from jax.experimental.pallas import tpu as pltpu
from jax.sharding import PartitionSpec as P

MESH = pl.DeviceIdType.MESH
RING = (0, 1, -1, 2)
LANES = 128
ORDER_X = (3, 1, 2, 0)
ORDER_Y = (3, 1, 2, 0)
ORDER_Z = (3, 1, 2, 0)
EARLY = 24
HALF = 256
CHUNKS = 1
STORES = 4


def split(value):
    high = value.astype(jnp.bfloat16).astype(jnp.float32)
    return high, value - high


def kernel(
    counts_hbm, nf_hbm, pf_hbm, tf_hbm, gn_ref, gp_ref, gt_ref,
    nf_ref, pf_ref, tf_ref, counts, stage, proj, part_a, sum_a, part_v, sum_v, mean_v, far_v, final,
    a1, a2, v1, v2, v3, other,
    factor_sem, counts_sem, a1_s, a1_r, a2_s, a2_r, a3_s, a3_r, a4_s, a4_r, v1_s, v1_r, v2_s, v2_r, v3_s, v3_r, v4_s, v4_r,
    plane_sem, cube_sem,
):
    ranks, i_dev = nf_ref.shape
    j_dev, k_dev = pf_ref.shape[1], tf_ref.shape[1]
    neurons = i_dev * lax.axis_size("neuron")
    positions = j_dev * lax.axis_size("pos")
    trials = k_dev * lax.axis_size("trial")
    chunks = counts.shape[0]
    k_chunk = k_dev // chunks
    rows = k_chunk * j_dev

    factors = []
    for at_sem, (src, dst) in enumerate(((pf_hbm, pf_ref), (tf_hbm, tf_ref), (nf_hbm, nf_ref))):
        load = pltpu.make_async_copy(src, dst, factor_sem.at[at_sem])
        load.start()
        factors.append(load)
    loads = []
    for chunk in range(chunks):
        load = pltpu.make_async_copy(
            counts_hbm.at[pl.ds(chunk * k_chunk, k_chunk)], counts.at[chunk], counts_sem.at[chunk]
        )
        load.start()
        loads.append(load)

    me, y, z_hi = lax.axis_index("neuron"), lax.axis_index("pos"), lax.axis_index("trial")
    core, x, z_lo = lax.rem(me, 2), lax.rem(me // 2, 4), me // 8
    z = z_hi * 4 + z_lo
    sign = 1 - 2 * core
    steps_z = (0, 1, -1, 2 * sign)
    xs = [lax.rem(x + 4 + d, 4) for d in RING]
    xs_back = [lax.rem(x + 4 - d, 4) for d in RING]
    ys = [lax.rem(y + 4 + d, 4) for d in RING]
    ys_back = [lax.rem(y + 4 - d, 4) for d in RING]
    zs = [lax.rem(z + 16 + d, 16) for d in steps_z]
    zs_back = [lax.rem(z + 16 - d, 16) for d in steps_z]
    his = [lax.rem(z_hi + 4 + d, 4) for d in RING]
    his_back = [lax.rem(z_hi + 4 - d, 4) for d in RING]

    def at(x_, y_, z_, core_):
        return {"neuron": (lax.rem(z_, 4) * 4 + x_) * 2 + core_, "pos": y_, "trial": z_ // 4}

    def column(x_, z_):
        return (lax.rem(z_, 4) * 4 + x_) * 2 * i_dev

    cube = [(a, b, c) for c in ORDER_Z for b in ORDER_Y for a in ORDER_X if a or b or c]

    barrier = pltpu.get_barrier_semaphore()
    greeted = [at(xs_back[a], y, z, core) for a in (1, 2, 3)]
    greeted += [at(xs_back[a], y, z, 1 - core) for a in range(4)]
    greeted += [at(x, ys_back[b], z, core) for b in (1, 2, 3)]
    greeted += [at(x, y, zs_back[c], core) for c in (1, 2, 3)]
    greeted += [at(x, y, zs[3], core)]
    greeted += [{"neuron": me, "pos": y, "trial": his_back[h]} for h in (1, 2, 3)]
    for device in greeted:
        pl.semaphore_signal(barrier, inc=1, device_id=device, device_id_type=MESH)

    for load in factors:
        load.wait()
    nf, pf, tf = nf_ref[...], pf_ref[...], tf_ref[...]
    stage[...] = jnp.zeros_like(stage)
    for group in range(4):
        stage[pl.ds(group * ranks, ranks), pl.ds(0, j_dev)] = pf
        stage[pl.ds(group * ranks, ranks), pl.ds(j_dev, k_dev)] = tf
    turned = stage[...].T
    pf_t, tf_t = turned[:j_dev], turned[j_dev : j_dev + k_dev]
    lane = lax.broadcasted_iota(jnp.int32, (j_dev, LANES), 1)
    use_high = lax.rem(lane // ranks, 2) == 0
    nf_high, nf_low = split(nf)
    blank = jnp.zeros((LANES - 4 * ranks, i_dev), jnp.float32)
    nf_model = jnp.concatenate([nf_high, nf_high, nf_low, nf_low, blank], axis=0).astype(jnp.bfloat16)
    blank = jnp.zeros((LANES - 2 * ranks, i_dev), jnp.float32)
    nf_proj = jnp.concatenate([nf_high, nf_low, blank], axis=0).T.astype(jnp.bfloat16)
    pf_pair = jnp.concatenate([pf, pf], axis=1)
    left = lax.broadcasted_iota(jnp.int32, (ranks, LANES), 1) < j_dev

    half = HALF
    acc = [jnp.zeros((2 * ranks, half), jnp.float32) for _ in range(i_dev // half)]
    weights_t, weights = [], []
    for k in range(k_dev):
        high, low = split(pf_t * tf_t[k : k + 1])
        weights_t.append(jnp.where(use_high, high, low).astype(jnp.bfloat16))
    for k in range(0, k_dev, 2):
        high, low = split(pf_pair * jnp.where(left, tf[:, k : k + 1], tf[:, k + 1 : k + 2]))
        weights.append(jnp.concatenate([high, low], axis=0).astype(jnp.bfloat16))
    for chunk in range(chunks):
        k0 = chunk * k_chunk
        chunk_t = jnp.concatenate(weights_t[k0 : k0 + k_chunk], axis=0)
        chunk_w = jnp.concatenate(weights[k0 // 2 : (k0 + k_chunk) // 2], axis=1)
        models = [
            jnp.dot(chunk_t, nf_model[:, part * half : (part + 1) * half], preferred_element_type=jnp.float32)
            for part in range(i_dev // half)
        ]
        loads[chunk].wait()
        projected = jnp.zeros((rows, LANES), jnp.float32)
        for part in range(i_dev // half):
            cols = slice(part * half, (part + 1) * half)
            model = models[part]
            guess = pl.reciprocal(model, approx=True)
            inverse = guess * (2.0 - model * guess)
            spikes = counts[chunk, :, :, cols].reshape(rows, half).astype(jnp.float32)
            ratio = 1.0 - spikes * inverse
            high = ratio.astype(jnp.bfloat16)
            low = (ratio - high.astype(jnp.float32)).astype(jnp.bfloat16)
            for piece in (high, low):
                acc[part] = acc[part] + jnp.dot(chunk_w, piece, preferred_element_type=jnp.float32)
                projected = projected + jnp.dot(piece, nf_proj[cols], preferred_element_type=jnp.float32)
        proj[pl.ds(k0 * j_dev, rows), :] = projected
    for part in range(i_dev // half):
        part_a[:, pl.ds(part * half, half)] = (acc[part][:ranks] + acc[part][ranks:]) / (positions * trials)

    pl.semaphore_wait(barrier, len(greeted))
    for a in (1, 2, 3):
        pl.semaphore_signal(plane_sem, inc=1, device_id=at(xs_back[a], y, z, core), device_id_type=MESH)

    def send(src, dst, send_sem, recv_sem, device):
        copy = pltpu.make_async_remote_copy(
            src_ref=src, dst_ref=dst, send_sem=send_sem, recv_sem=recv_sem, device_id=device, device_id_type=MESH
        )
        copy.start()
        return copy

    tall, wide = ranks // 2, i_dev // 2

    def quarter_of(ref, index, start):
        row, col = (index // 2) * tall, start + lax.rem(index, 2) * wide
        return ref.at[pl.ds(pl.multiple_of(row, tall), tall), pl.ds(pl.multiple_of(col, wide), wide)]

    first_a = [
        send(quarter_of(part_a, ys[d], 0), a1.at[d - 1], a1_s.at[d - 1], a1_r.at[d - 1], {"neuron": me, "pos": ys[d], "trial": z_hi})
        for d in (3, 1, 2)
    ]

    grad_b = jnp.zeros((j_dev, LANES), jnp.float32)
    grad_c = []
    for k in range(k_dev):
        block = proj[pl.ds(k * j_dev, j_dev), :]
        grad_b = grad_b + block * tf_t[k : k + 1]
        grad_c.append(jnp.sum(block * pf_t, axis=0, keepdims=True))
    stage[pl.ds(0, j_dev), :] = grad_b / (neurons * trials)
    stage[pl.ds(j_dev, LANES - j_dev), :] = jnp.zeros((LANES - j_dev, LANES), jnp.float32)
    stage[pl.ds(pl.multiple_of(j_dev + z_hi * k_dev, k_dev), k_dev), :] = jnp.concatenate(grad_c, axis=0) / (
        neurons * positions
    )
    turned = stage[...].T
    part_v[...] = (turned[:ranks] + turned[ranks : 2 * ranks]).reshape(part_v.shape)
    first_v = []
    for a in range(4):
        for c in range(2):
            if a or c:
                other_core = core if c == 0 else 1 - core
                slot = a * 2 + c - 1
                first_v.append(
                    send(part_v.at[other_core], v1.at[slot], v1_s.at[slot], v1_r.at[slot], at(xs[a], y, z, other_core))
                )

    for copy in first_a:
        copy.wait_recv()
    sum_a[...] = (a1[0] + a1[1]) + (a1[2] + quarter_of(part_a, y, 0)[...])
    second_a = [
        send(sum_a, a2.at[h - 1], a2_s.at[h - 1], a2_r.at[h - 1], {"neuron": me, "pos": y, "trial": his[h]})
        for h in (3, 1, 2)
    ]
    pl.semaphore_wait(plane_sem, 3)
    for c in (1, 2, 3):
        pl.semaphore_signal(cube_sem, inc=1, device_id=at(x, y, zs_back[c], core), device_id_type=MESH)
    for copy in first_v:
        copy.wait_recv()
    total = part_v[core]
    for slot in range(7):
        total = total + v1[slot]
    sum_v[...] = total
    second_v = [
        send(sum_v, v2.at[h - 1], v2_s.at[h - 1], v2_r.at[h - 1], {"neuron": me, "pos": y, "trial": his[h]})
        for h in (3, 1, 2)
    ]

    for copy in second_a:
        copy.wait_recv()
    mine = quarter_of(gn_ref, y, me * i_dev)
    mine[...] = (a2[0] + a2[1]) + (a2[2] + sum_a[...])
    pl.semaphore_wait(cube_sem, 3)

    def spread(steps):
        for a, b, c in steps:
            send(mine, mine, a3_s, a3_r.at[c * 4 + a], at(xs[a], ys[b], zs[c], core))

    spread(cube[:EARLY])
    for copy in second_v:
        copy.wait_recv()
    mean_v[...] = (v2[0] + v2[1]) + (v2[2] + sum_v[...])
    third_v = []
    for b in ORDER_Y:
        for c in ORDER_Z:
            if b or c:
                slot = c * 4 + b
                third_v.append(
                    send(mean_v, v3.at[slot], v3_s.at[slot], v3_r.at[slot], at(x, ys[b], zs[c], core))
                )
    spread(cube[EARLY:])
    v3[0] = mean_v[...]

    partner = {"neuron": me + sign, "pos": y, "trial": z_hi}

    def block_of(start):
        return gn_ref.at[:, pl.ds(pl.multiple_of(start, i_dev), i_dev)]

    fourth = []
    for c in ORDER_Z:
        for a in ORDER_X:
            slot = c * 4 + a
            block = block_of(column(xs_back[a], zs_back[c]) + core * i_dev)
            if slot == 0:
                landed = gn_ref.at[pl.ds(0, tall), pl.ds(0, 3 * wide)]
            else:
                landed = block
            pltpu.make_async_copy(landed, landed, a3_r.at[slot]).wait()
            fourth.append(send(block, block, a4_s.at[slot], a4_r.at[slot], partner))
    for copy in third_v:
        copy.wait_recv()
    all_c = jnp.zeros((8, LANES), jnp.float32)
    for b in range(4):
        over_z = (v3[b] + v3[4 + b]) + (v3[8 + b] + v3[12 + b])
        all_c = all_c + over_z
        far_v[ys_back[b]] = over_z
    final[4] = all_c
    for b in range(4):
        final[b] = far_v[b]
    swap = send(final, other, v4_s, v4_r, partner)

    def write(ref, row):
        for b in range(4):
            gp_ref[pl.ds(row, 8), pl.ds(b * j_dev, j_dev)] = ref[b][:, :j_dev]
        gt_ref[pl.ds(row, 8), :] = ref[4][:, j_dev:]

    write(final, pl.multiple_of(core * 8, 8))
    swap.wait_recv()
    write(other, pl.multiple_of((1 - core) * 8, 8))
    for copy in fourth:
        copy.wait_recv()

    for copy in first_a + first_v + second_a + second_v + third_v + fourth + [swap]:
        copy.wait_send()
    sent = gn_ref.at[pl.ds(0, tall), pl.ds(0, len(cube) * wide)]
    pltpu.make_async_copy(sent, sent, a3_s).wait()


def store(gn_ref, gp_ref, gt_ref, gn_hbm, gp_hbm, gt_hbm, sem):
    width = gn_ref.shape[1] // STORES
    copies = [
        pltpu.make_async_copy(gn_ref.at[:, pl.ds(i * width, width)], gn_hbm.at[:, pl.ds(i * width, width)], sem.at[i])
        for i in range(STORES)
    ]
    copies.append(pltpu.make_async_copy(gp_ref, gp_hbm, sem.at[STORES]))
    copies.append(pltpu.make_async_copy(gt_ref, gt_hbm, sem.at[STORES + 1]))
    for copy in copies:
        copy.start()
    for copy in copies:
        copy.wait()


def body(counts, neuron_factors, pos_factors, trial_factors):
    k_dev, j_dev, i_dev = counts.shape
    ranks = neuron_factors.shape[0]
    chunks = CHUNKS
    vmem = pl.BlockSpec(memory_space=pltpu.VMEM)
    f32 = jnp.float32
    dma = pltpu.SemaphoreType.DMA
    gathered = pl.pallas_call(
        kernel,
        name="gradients",
        out_shape=(
            pltpu.VMEM((ranks, i_dev * lax.axis_size("neuron")), f32),
            pltpu.VMEM((ranks, j_dev * lax.axis_size("pos")), f32),
            pltpu.VMEM((ranks, k_dev * lax.axis_size("trial")), f32),
        ),
        in_specs=[pl.BlockSpec(memory_space=pltpu.HBM)] * 4,
        out_specs=(vmem, vmem, vmem),
        scratch_shapes=[
            pltpu.VMEM((ranks, i_dev), f32),
            pltpu.VMEM((ranks, j_dev), f32),
            pltpu.VMEM((ranks, k_dev), f32),
            pltpu.VMEM((chunks, k_dev // chunks, j_dev, i_dev), jnp.int32),
            pltpu.VMEM((LANES, LANES), f32),
            pltpu.VMEM((k_dev * j_dev, LANES), f32),
            pltpu.VMEM((ranks, i_dev), f32),
            pltpu.VMEM((ranks // 2, i_dev // 2), f32),
            pltpu.VMEM((2, 8, LANES), f32),
            pltpu.VMEM((8, LANES), f32),
            pltpu.VMEM((8, LANES), f32),
            pltpu.VMEM((4, 8, LANES), f32),
            pltpu.VMEM((5, 8, LANES), f32),
            pltpu.VMEM((3, ranks // 2, i_dev // 2), f32),
            pltpu.VMEM((3, ranks // 2, i_dev // 2), f32),
            pltpu.VMEM((7, 8, LANES), f32),
            pltpu.VMEM((3, 8, LANES), f32),
            pltpu.VMEM((16, 8, LANES), f32),
            pltpu.VMEM((5, 8, LANES), f32),
            dma((3,)), dma((chunks,)),
            dma((3,)), dma((3,)), dma((3,)), dma((3,)),
            dma, dma((16,)), dma((16,)), dma((16,)),
            dma((7,)), dma((7,)), dma((3,)), dma((3,)),
            dma((16,)), dma((16,)), dma, dma,
            pltpu.SemaphoreType.REGULAR, pltpu.SemaphoreType.REGULAR,
        ],
        compiler_params=pltpu.CompilerParams(
            collective_id=0, has_side_effects=True, vmem_limit_bytes=32 << 20
        ),
    )(*(pltpu.with_memory_space_constraint(one, pltpu.HBM) for one in (counts, neuron_factors, pos_factors, trial_factors)))
    return pl.pallas_call(
        store,
        name="store",
        out_shape=tuple(jax.ShapeDtypeStruct(one.shape, f32) for one in gathered),
        in_specs=[vmem] * 3,
        out_specs=(pl.BlockSpec(memory_space=pltpu.HBM),) * 3,
        scratch_shapes=[dma((STORES + 2,))],
    )(*(pltpu.with_memory_space_constraint(one, pltpu.VMEM) for one in gathered))


def solution(mesh):
    placed = (P("trial", "pos", "neuron"), P(None, "neuron"), P(None, "pos"), P(None, "trial"))
    return jax.shard_map(
        body, mesh=mesh, in_specs=placed, out_specs=(P(), P(), P()), check_vma=False
    )
```

```python
import jax
import jax.numpy as jnp
from jax import lax
from jax.experimental import pallas as pl
from jax.experimental.pallas import tpu as pltpu
from jax.sharding import PartitionSpec as P

MESH = pl.DeviceIdType.MESH
RING = (0, 1, -1, 2)
LANES = 128
ORDER_X = (3, 1, 2, 0)
ORDER_Y = (3, 1, 2, 0)
ORDER_Z = (0, 1, 3, 2)
VTURN = 3
VFIN = 15
LOADS = 8
HALF = 256
CHUNKS = 1
STORES = 4


def split(value):
    high = value.astype(jnp.bfloat16).astype(jnp.float32)
    return high, value - high


def kernel(
    counts_hbm, nf_hbm, pf_hbm, tf_hbm, gn_ref, gp_ref, gt_ref,
    nf_ref, pf_ref, tf_ref, counts, stage, proj, part_a, sum_a, part_v, sum_v, mean_v, final,
    a1, a2, v1, v2, v3, other,
    factor_sem, counts_sem, a1_s, a1_r, a2_s, a2_r, a3_s, a3_r, a4_s, a4_r, v1_s, v1_r, v2_s, v2_r, v3_s, v3_r, v4_s, v4_r,
    plane_sem, cube_sem,
):
    ranks, i_dev = nf_ref.shape
    j_dev, k_dev = pf_ref.shape[1], tf_ref.shape[1]
    neurons = i_dev * lax.axis_size("neuron")
    positions = j_dev * lax.axis_size("pos")
    trials = k_dev * lax.axis_size("trial")
    chunks = CHUNKS
    k_chunk = k_dev // chunks
    rows = k_chunk * j_dev

    factors = []
    for at_sem, (src, dst) in enumerate(((pf_hbm, pf_ref), (tf_hbm, tf_ref), (nf_hbm, nf_ref))):
        load = pltpu.make_async_copy(src, dst, factor_sem.at[at_sem])
        load.start()
        factors.append(load)
    loads = []
    step = k_dev // LOADS
    for part in range(LOADS):
        load = pltpu.make_async_copy(
            counts_hbm.at[pl.ds(part * step, step)], counts.at[pl.ds(part * step, step)], counts_sem.at[part]
        )
        load.start()
        loads.append(load)

    me, y, z_hi = lax.axis_index("neuron"), lax.axis_index("pos"), lax.axis_index("trial")
    core, x, z_lo = lax.rem(me, 2), lax.rem(me // 2, 4), me // 8
    z = z_hi * 4 + z_lo
    sign = 1 - 2 * core
    steps_z = (0, 1, 2 * sign, -1)
    xs = [lax.rem(x + 4 + d, 4) for d in RING]
    xs_back = [lax.rem(x + 4 - d, 4) for d in RING]
    ys = [lax.rem(y + 4 + d, 4) for d in RING]
    ys_back = [lax.rem(y + 4 - d, 4) for d in RING]
    zs = [lax.rem(z + 16 + d, 16) for d in steps_z]
    zs_back = [lax.rem(z + 16 - d, 16) for d in steps_z]
    his = [lax.rem(z_hi + 4 + d, 4) for d in RING]
    his_back = [lax.rem(z_hi + 4 - d, 4) for d in RING]

    def at(x_, y_, z_, core_):
        return {"neuron": (lax.rem(z_, 4) * 4 + x_) * 2 + core_, "pos": y_, "trial": z_ // 4}

    def column(x_, z_):
        return (lax.rem(z_, 4) * 4 + x_) * 2 * i_dev

    barrier = pltpu.get_barrier_semaphore()
    greeted = [at(xs_back[a], y, z, core) for a in (1, 2, 3)]
    greeted += [at(xs_back[a], y, z, 1 - core) for a in range(4)]
    greeted += [at(x, ys_back[b], z, core) for b in (1, 2, 3)]
    greeted += [at(x, y, zs_back[c], core) for c in (1, 2, 3)]
    greeted += [at(x, y, zs[2], core)]
    greeted += [{"neuron": me, "pos": y, "trial": his_back[h]} for h in (1, 2, 3)]
    for device in greeted:
        pl.semaphore_signal(barrier, inc=1, device_id=device, device_id_type=MESH)

    for load in factors:
        load.wait()
    nf, pf, tf = nf_ref[...], pf_ref[...], tf_ref[...]
    stage[...] = jnp.zeros_like(stage)
    for group in range(4):
        stage[pl.ds(group * ranks, ranks), pl.ds(0, j_dev)] = pf
        stage[pl.ds(group * ranks, ranks), pl.ds(j_dev, k_dev)] = tf
    turned = stage[...].T
    pf_t, tf_t = turned[:j_dev], turned[j_dev : j_dev + k_dev]
    lane = lax.broadcasted_iota(jnp.int32, (j_dev, LANES), 1)
    use_high = lax.rem(lane // ranks, 2) == 0
    nf_high, nf_low = split(nf)
    blank = jnp.zeros((LANES - 4 * ranks, i_dev), jnp.float32)
    nf_model = jnp.concatenate([nf_high, nf_high, nf_low, nf_low, blank], axis=0).astype(jnp.bfloat16)
    blank = jnp.zeros((LANES - 2 * ranks, i_dev), jnp.float32)
    nf_proj = jnp.concatenate([nf_high, nf_low, blank], axis=0).T.astype(jnp.bfloat16)
    pf_pair = jnp.concatenate([pf, pf], axis=1)
    left = lax.broadcasted_iota(jnp.int32, (ranks, LANES), 1) < j_dev

    half = HALF
    acc = [jnp.zeros((2 * ranks, half), jnp.float32) for _ in range(i_dev // half)]
    weights_t, weights = [], []
    for k in range(k_dev):
        high, low = split(pf_t * tf_t[k : k + 1])
        weights_t.append(jnp.where(use_high, high, low).astype(jnp.bfloat16))
    for k in range(0, k_dev, 2):
        high, low = split(pf_pair * jnp.where(left, tf[:, k : k + 1], tf[:, k + 1 : k + 2]))
        weights.append(jnp.concatenate([high, low], axis=0).astype(jnp.bfloat16))
    for chunk in range(chunks):
        k0 = chunk * k_chunk
        chunk_t = jnp.concatenate(weights_t[k0 : k0 + k_chunk], axis=0)
        chunk_w = jnp.concatenate(weights[k0 // 2 : (k0 + k_chunk) // 2], axis=1)
        models = [
            jnp.dot(chunk_t, nf_model[:, part * half : (part + 1) * half], preferred_element_type=jnp.float32)
            for part in range(i_dev // half)
        ]
        for load in loads[chunk * LOADS // chunks : (chunk + 1) * LOADS // chunks]:
            load.wait()
        projected = jnp.zeros((rows, LANES), jnp.float32)
        for part in range(i_dev // half):
            cols = slice(part * half, (part + 1) * half)
            model = models[part]
            guess = pl.reciprocal(model, approx=True)
            inverse = guess * (2.0 - model * guess)
            spikes = counts[k0 : k0 + k_chunk, :, cols].reshape(rows, half).astype(jnp.float32)
            ratio = 1.0 - spikes * inverse
            high = ratio.astype(jnp.bfloat16)
            low = (ratio - high.astype(jnp.float32)).astype(jnp.bfloat16)
            for piece in (high, low):
                acc[part] = acc[part] + jnp.dot(chunk_w, piece, preferred_element_type=jnp.float32)
                projected = projected + jnp.dot(piece, nf_proj[cols], preferred_element_type=jnp.float32)
        proj[pl.ds(k0 * j_dev, rows), :] = projected
    for part in range(i_dev // half):
        part_a[:, pl.ds(part * half, half)] = (acc[part][:ranks] + acc[part][ranks:]) / (positions * trials)

    pl.semaphore_wait(barrier, len(greeted))
    for a in (1, 2, 3):
        pl.semaphore_signal(plane_sem, inc=1, device_id=at(xs_back[a], y, z, core), device_id_type=MESH)

    def send(src, dst, send_sem, recv_sem, device):
        copy = pltpu.make_async_remote_copy(
            src_ref=src, dst_ref=dst, send_sem=send_sem, recv_sem=recv_sem, device_id=device, device_id_type=MESH
        )
        copy.start()
        return copy

    tall, wide = ranks // 2, i_dev // 2

    def quarter_of(ref, index, start):
        row, col = (index // 2) * tall, start + lax.rem(index, 2) * wide
        return ref.at[pl.ds(pl.multiple_of(row, tall), tall), pl.ds(pl.multiple_of(col, wide), wide)]

    first_a = [
        send(quarter_of(part_a, ys[d], 0), a1.at[d - 1], a1_s.at[d - 1], a1_r.at[d - 1], {"neuron": me, "pos": ys[d], "trial": z_hi})
        for d in (3, 1, 2)
    ]

    grad_b = jnp.zeros((j_dev, LANES), jnp.float32)
    grad_c = []
    for k in range(k_dev):
        block = proj[pl.ds(k * j_dev, j_dev), :]
        grad_b = grad_b + block * tf_t[k : k + 1]
        grad_c.append(jnp.sum(block * pf_t, axis=0, keepdims=True))
    stage[pl.ds(0, j_dev), :] = grad_b / (neurons * trials)
    stage[pl.ds(j_dev, LANES - j_dev), :] = jnp.zeros((LANES - j_dev, LANES), jnp.float32)
    stage[pl.ds(pl.multiple_of(j_dev + z_hi * k_dev, k_dev), k_dev), :] = jnp.concatenate(grad_c, axis=0) / (
        neurons * positions
    )
    turned = stage[...].T
    part_v[...] = (turned[:ranks] + turned[ranks : 2 * ranks]).reshape(part_v.shape)
    first_v = []
    for a in range(4):
        for c in range(2):
            if a or c:
                other_core = core if c == 0 else 1 - core
                slot = a * 2 + c - 1
                first_v.append(
                    send(part_v.at[other_core], v1.at[slot], v1_s.at[slot], v1_r.at[slot], at(xs[a], y, z, other_core))
                )

    for copy in first_a:
        copy.wait_recv()
    sum_a[...] = (a1[0] + a1[1]) + (a1[2] + quarter_of(part_a, y, 0)[...])
    second_a = [
        send(sum_a, a2.at[h - 1], a2_s.at[h - 1], a2_r.at[h - 1], {"neuron": me, "pos": y, "trial": his[h]})
        for h in (3, 1, 2)
    ]
    pl.semaphore_wait(plane_sem, 3)
    for c in (1, 2, 3):
        pl.semaphore_signal(cube_sem, inc=1, device_id=at(x, y, zs_back[c], core), device_id_type=MESH)
    for copy in first_v:
        copy.wait_recv()
    total = part_v[core]
    for slot in range(7):
        total = total + v1[slot]
    sum_v[...] = total
    second_v = [
        send(sum_v, v2.at[h - 1], v2_s.at[h - 1], v2_r.at[h - 1], {"neuron": me, "pos": y, "trial": his[h]})
        for h in (3, 1, 2)
    ]

    for copy in second_a:
        copy.wait_recv()
    mine = quarter_of(gn_ref, y, me * i_dev)
    mine[...] = (a2[0] + a2[1]) + (a2[2] + sum_a[...])
    pl.semaphore_wait(cube_sem, 3)

    below = -1 - core
    lowest = lax.rem(z + below + 16, 16)
    first = jnp.where(lowest > 12, 16 - lowest, 0)
    for turn in range(4):
        dz = lax.rem(first + turn, 4) + below
        z_to, c = lax.rem(z + dz + 16, 16), lax.rem(dz + 4, 4)
        for a in ORDER_X:
            for b in ORDER_Y:

                def give(a=a, b=b, c=c, z_to=z_to):
                    send(mine, mine, a3_s, a3_r.at[c * 4 + a], at(xs[a], ys[b], z_to, core))

                if a or b:
                    give()
                else:
                    pl.when(dz != 0)(give)
        if turn == VTURN:
            for copy in second_v:
                copy.wait_recv()
            mean_v[...] = (v2[0] + v2[1]) + (v2[2] + sum_v[...])
            v3[0] = mean_v[...]
        for late in range(turn + 1) if turn == VTURN else (turn,) if turn > VTURN else ():
            dz = lax.rem(first + late, 4) + below
            z_to, c = lax.rem(z + dz + 16, 16), lax.rem(dz + 4, 4)
            for b in ORDER_Y:

                def give_v(b=b, c=c, z_to=z_to):
                    slot = c * 4 + b
                    send(mean_v, v3.at[slot], v3_s, v3_r.at[slot], at(x, ys[b], z_to, core))

                if b:
                    give_v()
                else:
                    pl.when(dz != 0)(give_v)

    partner = {"neuron": me + sign, "pos": y, "trial": z_hi}

    def block_of(start):
        return gn_ref.at[:, pl.ds(pl.multiple_of(start, i_dev), i_dev)]

    def write(ref, row):
        for b in range(4):
            gp_ref[pl.ds(row, 8), pl.ds(b * j_dev, j_dev)] = ref[b][:, :j_dev]
        gt_ref[pl.ds(row, 8), :] = ref[4][:, j_dev:]

    fourth = []
    for turn, (a, c) in enumerate((a, c) for a in ORDER_X for c in ORDER_Z):
        if turn == VFIN:
            for slot in range(1, 16):
                pltpu.make_async_copy(v3.at[slot], v3.at[slot], v3_r.at[slot]).wait()
            all_c = jnp.zeros((8, LANES), jnp.float32)
            for b in range(4):
                over_z = (v3[b] + v3[4 + b]) + (v3[8 + b] + v3[12 + b])
                all_c = all_c + over_z
                final[ys_back[b]] = over_z
            final[4] = all_c
            swap = send(final, other, v4_s, v4_r, partner)
            write(final, pl.multiple_of(core * 8, 8))
        slot = c * 4 + a
        block = block_of(column(xs_back[a], zs_back[c]) + core * i_dev)
        if slot == 0:
            landed = gn_ref.at[pl.ds(0, tall), pl.ds(0, 3 * wide)]
        else:
            landed = block
        pltpu.make_async_copy(landed, landed, a3_r.at[slot]).wait()
        fourth.append(send(block, block, a4_s.at[slot], a4_r.at[slot], partner))
    swap.wait_recv()
    write(other, pl.multiple_of((1 - core) * 8, 8))
    for copy in fourth:
        copy.wait_recv()

    for copy in first_a + first_v + second_a + second_v + fourth + [swap]:
        copy.wait_send()
    sent = gn_ref.at[pl.ds(0, tall), pl.ds(0, 63 * wide)]
    pltpu.make_async_copy(sent, sent, a3_s).wait()
    pltpu.make_async_copy(v3.at[pl.ds(0, 15)], v3.at[pl.ds(0, 15)], v3_s).wait()


def store(gn_ref, gp_ref, gt_ref, gn_hbm, gp_hbm, gt_hbm, sem):
    width = gn_ref.shape[1] // STORES
    copies = [
        pltpu.make_async_copy(gn_ref.at[:, pl.ds(i * width, width)], gn_hbm.at[:, pl.ds(i * width, width)], sem.at[i])
        for i in range(STORES)
    ]
    copies.append(pltpu.make_async_copy(gp_ref, gp_hbm, sem.at[STORES]))
    copies.append(pltpu.make_async_copy(gt_ref, gt_hbm, sem.at[STORES + 1]))
    for copy in copies:
        copy.start()
    for copy in copies:
        copy.wait()


def body(counts, neuron_factors, pos_factors, trial_factors):
    k_dev, j_dev, i_dev = counts.shape
    ranks = neuron_factors.shape[0]
    vmem = pl.BlockSpec(memory_space=pltpu.VMEM)
    f32 = jnp.float32
    dma = pltpu.SemaphoreType.DMA
    gathered = pl.pallas_call(
        kernel,
        name="gradients",
        out_shape=(
            pltpu.VMEM((ranks, i_dev * lax.axis_size("neuron")), f32),
            pltpu.VMEM((ranks, j_dev * lax.axis_size("pos")), f32),
            pltpu.VMEM((ranks, k_dev * lax.axis_size("trial")), f32),
        ),
        in_specs=[pl.BlockSpec(memory_space=pltpu.HBM)] * 4,
        out_specs=(vmem, vmem, vmem),
        scratch_shapes=[
            pltpu.VMEM((ranks, i_dev), f32),
            pltpu.VMEM((ranks, j_dev), f32),
            pltpu.VMEM((ranks, k_dev), f32),
            pltpu.VMEM((k_dev, j_dev, i_dev), jnp.int32),
            pltpu.VMEM((LANES, LANES), f32),
            pltpu.VMEM((k_dev * j_dev, LANES), f32),
            pltpu.VMEM((ranks, i_dev), f32),
            pltpu.VMEM((ranks // 2, i_dev // 2), f32),
            pltpu.VMEM((2, 8, LANES), f32),
            pltpu.VMEM((8, LANES), f32),
            pltpu.VMEM((8, LANES), f32),
            pltpu.VMEM((5, 8, LANES), f32),
            pltpu.VMEM((3, ranks // 2, i_dev // 2), f32),
            pltpu.VMEM((3, ranks // 2, i_dev // 2), f32),
            pltpu.VMEM((7, 8, LANES), f32),
            pltpu.VMEM((3, 8, LANES), f32),
            pltpu.VMEM((16, 8, LANES), f32),
            pltpu.VMEM((5, 8, LANES), f32),
            dma((3,)), dma((LOADS,)),
            dma((3,)), dma((3,)), dma((3,)), dma((3,)),
            dma, dma((16,)), dma((16,)), dma((16,)),
            dma((7,)), dma((7,)), dma((3,)), dma((3,)),
            dma, dma((16,)), dma, dma,
            pltpu.SemaphoreType.REGULAR, pltpu.SemaphoreType.REGULAR,
        ],
        compiler_params=pltpu.CompilerParams(
            collective_id=0, has_side_effects=True, vmem_limit_bytes=32 << 20
        ),
    )(*(pltpu.with_memory_space_constraint(one, pltpu.HBM) for one in (counts, neuron_factors, pos_factors, trial_factors)))
    return pl.pallas_call(
        store,
        name="store",
        out_shape=tuple(jax.ShapeDtypeStruct(one.shape, f32) for one in gathered),
        in_specs=[vmem] * 3,
        out_specs=(pl.BlockSpec(memory_space=pltpu.HBM),) * 3,
        scratch_shapes=[dma((STORES + 2,))],
    )(*(pltpu.with_memory_space_constraint(one, pltpu.VMEM) for one in gathered))


def solution(mesh):
    placed = (P("trial", "pos", "neuron"), P(None, "neuron"), P(None, "pos"), P(None, "trial"))
    return jax.shard_map(
        body, mesh=mesh, in_specs=placed, out_specs=(P(), P(), P()), check_vma=False
    )
```

```python
import jax
import jax.numpy as jnp
from jax import lax
from jax.experimental import pallas as pl
from jax.experimental.pallas import tpu as pltpu
from jax.sharding import PartitionSpec as P

MESH = pl.DeviceIdType.MESH
RING = (0, 1, -1, 2)
LANES = 128
ORDER_X = (3, 1, 2, 0)
ORDER_Y = (3, 1, 2, 0)
ORDER_Z = (0, 1, 3, 2)
VTURN = 3
VFIN = 15
LOADS = 8
HALF = 256
CHUNKS = 1
STORES = 4


def split(value):
    high = value.astype(jnp.bfloat16).astype(jnp.float32)
    return high, value - high


def kernel(
    counts_hbm, nf_hbm, pf_hbm, tf_hbm, gn_ref, gp_ref, gt_ref,
    nf_ref, pf_ref, tf_ref, counts, stage, proj, part_a, sum_a, part_v, sum_v, mean_v, final,
    a1, a2, v1, v2, v3, other,
    factor_sem, counts_sem, a1_s, a1_r, a2_s, a2_r, a3_s, a3_r, a4_s, a4_r, v1_s, v1_r, v2_s, v2_r, v3_s, v3_r, v4_s, v4_r,
    plane_sem, cube_sem, link_sem,
):
    ranks, i_dev = nf_ref.shape
    j_dev, k_dev = pf_ref.shape[1], tf_ref.shape[1]
    neurons = i_dev * lax.axis_size("neuron")
    positions = j_dev * lax.axis_size("pos")
    trials = k_dev * lax.axis_size("trial")
    chunks = CHUNKS
    k_chunk = k_dev // chunks
    rows = k_chunk * j_dev

    factors = []
    for at_sem, (src, dst) in enumerate(((pf_hbm, pf_ref), (tf_hbm, tf_ref), (nf_hbm, nf_ref))):
        load = pltpu.make_async_copy(src, dst, factor_sem.at[at_sem])
        load.start()
        factors.append(load)
    loads = []
    step = k_dev // LOADS
    for part in range(LOADS):
        load = pltpu.make_async_copy(
            counts_hbm.at[pl.ds(part * step, step)], counts.at[pl.ds(part * step, step)], counts_sem.at[part]
        )
        load.start()
        loads.append(load)

    me, y, z_hi = lax.axis_index("neuron"), lax.axis_index("pos"), lax.axis_index("trial")
    core, x, z_lo = lax.rem(me, 2), lax.rem(me // 2, 4), me // 8
    z = z_hi * 4 + z_lo
    sign = 1 - 2 * core
    steps_z = (0, 1, 2 * sign, -1)
    xs = [lax.rem(x + 4 + d, 4) for d in RING]
    xs_back = [lax.rem(x + 4 - d, 4) for d in RING]
    ys = [lax.rem(y + 4 + d, 4) for d in RING]
    ys_back = [lax.rem(y + 4 - d, 4) for d in RING]
    zs = [lax.rem(z + 16 + d, 16) for d in steps_z]
    zs_back = [lax.rem(z + 16 - d, 16) for d in steps_z]
    his = [lax.rem(z_hi + 4 + d, 4) for d in RING]
    his_back = [lax.rem(z_hi + 4 - d, 4) for d in RING]

    def at(x_, y_, z_, core_):
        return {"neuron": (lax.rem(z_, 4) * 4 + x_) * 2 + core_, "pos": y_, "trial": z_ // 4}

    def column(x_, z_):
        return (lax.rem(z_, 4) * 4 + x_) * 2 * i_dev

    barrier = pltpu.get_barrier_semaphore()
    greeted = [at(xs[a], y, z, 0) for a in (1, 2, 3)] + [at(x, ys[b], z, 0) for b in (1, 2, 3)]
    greeted += [at(x, y, lax.rem(z + 16 + d, 16), 1) for d in (8, 4, -4, 2, -2, 1, -1)]
    for device in greeted:
        pl.semaphore_signal(barrier, inc=1, device_id=device, device_id_type=MESH)

    def greet_core():
        pl.semaphore_signal(barrier, inc=1, device_id=at(x, y, z, 0), device_id_type=MESH)

    pl.when(core == 1)(greet_core)

    for load in factors:
        load.wait()
    nf, pf, tf = nf_ref[...], pf_ref[...], tf_ref[...]
    stage[...] = jnp.zeros_like(stage)
    for group in range(4):
        stage[pl.ds(group * ranks, ranks), pl.ds(0, j_dev)] = pf
        stage[pl.ds(group * ranks, ranks), pl.ds(j_dev, k_dev)] = tf
    turned = stage[...].T
    pf_t, tf_t = turned[:j_dev], turned[j_dev : j_dev + k_dev]
    lane = lax.broadcasted_iota(jnp.int32, (j_dev, LANES), 1)
    use_high = lax.rem(lane // ranks, 2) == 0
    nf_high, nf_low = split(nf)
    blank = jnp.zeros((LANES - 4 * ranks, i_dev), jnp.float32)
    nf_model = jnp.concatenate([nf_high, nf_high, nf_low, nf_low, blank], axis=0).astype(jnp.bfloat16)
    blank = jnp.zeros((LANES - 2 * ranks, i_dev), jnp.float32)
    nf_proj = jnp.concatenate([nf_high, nf_low, blank], axis=0).T.astype(jnp.bfloat16)
    pf_pair = jnp.concatenate([pf, pf], axis=1)
    left = lax.broadcasted_iota(jnp.int32, (ranks, LANES), 1) < j_dev

    half = HALF
    acc = [jnp.zeros((2 * ranks, half), jnp.float32) for _ in range(i_dev // half)]
    weights_t, weights = [], []
    for k in range(k_dev):
        high, low = split(pf_t * tf_t[k : k + 1])
        weights_t.append(jnp.where(use_high, high, low).astype(jnp.bfloat16))
    for k in range(0, k_dev, 2):
        high, low = split(pf_pair * jnp.where(left, tf[:, k : k + 1], tf[:, k + 1 : k + 2]))
        weights.append(jnp.concatenate([high, low], axis=0).astype(jnp.bfloat16))
    for chunk in range(chunks):
        k0 = chunk * k_chunk
        chunk_t = jnp.concatenate(weights_t[k0 : k0 + k_chunk], axis=0)
        chunk_w = jnp.concatenate(weights[k0 // 2 : (k0 + k_chunk) // 2], axis=1)
        models = [
            jnp.dot(chunk_t, nf_model[:, part * half : (part + 1) * half], preferred_element_type=jnp.float32)
            for part in range(i_dev // half)
        ]
        for load in loads[chunk * LOADS // chunks : (chunk + 1) * LOADS // chunks]:
            load.wait()
        projected = jnp.zeros((rows, LANES), jnp.float32)
        for part in range(i_dev // half):
            cols = slice(part * half, (part + 1) * half)
            model = models[part]
            guess = pl.reciprocal(model, approx=True)
            inverse = guess * (2.0 - model * guess)
            spikes = counts[k0 : k0 + k_chunk, :, cols].reshape(rows, half).astype(jnp.float32)
            ratio = 1.0 - spikes * inverse
            high = ratio.astype(jnp.bfloat16)
            low = (ratio - high.astype(jnp.float32)).astype(jnp.bfloat16)
            for piece in (high, low):
                acc[part] = acc[part] + jnp.dot(chunk_w, piece, preferred_element_type=jnp.float32)
                projected = projected + jnp.dot(piece, nf_proj[cols], preferred_element_type=jnp.float32)
        proj[pl.ds(k0 * j_dev, rows), :] = projected
    for part in range(i_dev // half):
        part_a[:, pl.ds(part * half, half)] = (acc[part][:ranks] + acc[part][ranks:]) / (positions * trials)

    def hear(count):
        pl.semaphore_wait(barrier, count)
        pl.semaphore_signal(link_sem, inc=1, device_id=at(x, y, z, 1 - core), device_id_type=MESH)

    def told():
        pl.semaphore_wait(link_sem, 1)

    pl.when(core == 0)(lambda: hear(13))
    pl.when(core == 1)(told)
    for a in (1, 2, 3):
        pl.semaphore_signal(plane_sem, inc=1, device_id=at(xs_back[a], y, z, core), device_id_type=MESH)

    def send(src, dst, send_sem, recv_sem, device):
        copy = pltpu.make_async_remote_copy(
            src_ref=src, dst_ref=dst, send_sem=send_sem, recv_sem=recv_sem, device_id=device, device_id_type=MESH
        )
        copy.start()
        return copy

    tall, wide = ranks // 2, i_dev // 2

    def quarter_of(ref, index, start):
        row, col = (index // 2) * tall, start + lax.rem(index, 2) * wide
        return ref.at[pl.ds(pl.multiple_of(row, tall), tall), pl.ds(pl.multiple_of(col, wide), wide)]

    first_a = [
        send(quarter_of(part_a, ys[d], 0), a1.at[d - 1], a1_s.at[d - 1], a1_r.at[d - 1], {"neuron": me, "pos": ys[d], "trial": z_hi})
        for d in (3, 1, 2)
    ]

    grad_b = jnp.zeros((j_dev, LANES), jnp.float32)
    grad_c = []
    for k in range(k_dev):
        block = proj[pl.ds(k * j_dev, j_dev), :]
        grad_b = grad_b + block * tf_t[k : k + 1]
        grad_c.append(jnp.sum(block * pf_t, axis=0, keepdims=True))
    stage[pl.ds(0, j_dev), :] = grad_b / (neurons * trials)
    stage[pl.ds(j_dev, LANES - j_dev), :] = jnp.zeros((LANES - j_dev, LANES), jnp.float32)
    stage[pl.ds(pl.multiple_of(j_dev + z_hi * k_dev, k_dev), k_dev), :] = jnp.concatenate(grad_c, axis=0) / (
        neurons * positions
    )
    turned = stage[...].T
    part_v[...] = (turned[:ranks] + turned[ranks : 2 * ranks]).reshape(part_v.shape)
    first_v = []
    for a in range(4):
        for c in range(2):
            if a or c:
                other_core = core if c == 0 else 1 - core
                slot = a * 2 + c - 1
                first_v.append(
                    send(part_v.at[other_core], v1.at[slot], v1_s.at[slot], v1_r.at[slot], at(xs[a], y, z, other_core))
                )

    for copy in first_a:
        copy.wait_recv()
    sum_a[...] = (a1[0] + a1[1]) + (a1[2] + quarter_of(part_a, y, 0)[...])
    pl.when(core == 1)(lambda: hear(14))
    pl.when(core == 0)(told)
    second_a = [
        send(sum_a, a2.at[h - 1], a2_s.at[h - 1], a2_r.at[h - 1], {"neuron": me, "pos": y, "trial": his[h]})
        for h in (3, 1, 2)
    ]
    pl.semaphore_wait(plane_sem, 3)
    for c in (1, 2, 3):
        pl.semaphore_signal(cube_sem, inc=1, device_id=at(x, y, zs_back[c], core), device_id_type=MESH)
    for copy in first_v:
        copy.wait_recv()
    total = part_v[core]
    for slot in range(7):
        total = total + v1[slot]
    sum_v[...] = total
    second_v = [
        send(sum_v, v2.at[h - 1], v2_s.at[h - 1], v2_r.at[h - 1], {"neuron": me, "pos": y, "trial": his[h]})
        for h in (3, 1, 2)
    ]

    for copy in second_a:
        copy.wait_recv()
    mine = quarter_of(gn_ref, y, me * i_dev)
    mine[...] = (a2[0] + a2[1]) + (a2[2] + sum_a[...])
    pl.semaphore_wait(cube_sem, 3)

    below = -1 - core
    lowest = lax.rem(z + below + 16, 16)
    first = jnp.where(lowest > 12, 16 - lowest, 0)
    for turn in range(4):
        dz = lax.rem(first + turn, 4) + below
        z_to, c = lax.rem(z + dz + 16, 16), lax.rem(dz + 4, 4)
        for a in ORDER_X:
            for b in ORDER_Y:

                def give(a=a, b=b, c=c, z_to=z_to):
                    send(mine, mine, a3_s, a3_r.at[c * 4 + a], at(xs[a], ys[b], z_to, core))

                if a or b:
                    give()
                else:
                    pl.when(dz != 0)(give)
        if turn == VTURN:
            for copy in second_v:
                copy.wait_recv()
            mean_v[...] = (v2[0] + v2[1]) + (v2[2] + sum_v[...])
            v3[0] = mean_v[...]
        for late in range(turn + 1) if turn == VTURN else (turn,) if turn > VTURN else ():
            dz = lax.rem(first + late, 4) + below
            z_to, c = lax.rem(z + dz + 16, 16), lax.rem(dz + 4, 4)
            for b in ORDER_Y:

                def give_v(b=b, c=c, z_to=z_to):
                    slot = c * 4 + b
                    send(mean_v, v3.at[slot], v3_s, v3_r.at[slot], at(x, ys[b], z_to, core))

                if b:
                    give_v()
                else:
                    pl.when(dz != 0)(give_v)

    partner = {"neuron": me + sign, "pos": y, "trial": z_hi}

    def block_of(start):
        return gn_ref.at[:, pl.ds(pl.multiple_of(start, i_dev), i_dev)]

    def write(ref, row):
        for b in range(4):
            gp_ref[pl.ds(row, 8), pl.ds(b * j_dev, j_dev)] = ref[b][:, :j_dev]
        gt_ref[pl.ds(row, 8), :] = ref[4][:, j_dev:]

    fourth = []
    for turn, (a, c) in enumerate((a, c) for a in ORDER_X for c in ORDER_Z):
        if turn == VFIN:
            for slot in range(1, 16):
                pltpu.make_async_copy(v3.at[slot], v3.at[slot], v3_r.at[slot]).wait()
            all_c = jnp.zeros((8, LANES), jnp.float32)
            for b in range(4):
                over_z = (v3[b] + v3[4 + b]) + (v3[8 + b] + v3[12 + b])
                all_c = all_c + over_z
                final[ys_back[b]] = over_z
            final[4] = all_c
            swap = send(final, other, v4_s, v4_r, partner)
            write(final, pl.multiple_of(core * 8, 8))
        slot = c * 4 + a
        block = block_of(column(xs_back[a], zs_back[c]) + core * i_dev)
        if slot == 0:
            landed = gn_ref.at[pl.ds(0, tall), pl.ds(0, 3 * wide)]
        else:
            landed = block
        pltpu.make_async_copy(landed, landed, a3_r.at[slot]).wait()
        fourth.append(send(block, block, a4_s.at[slot], a4_r.at[slot], partner))
    swap.wait_recv()
    write(other, pl.multiple_of((1 - core) * 8, 8))
    for copy in fourth:
        copy.wait_recv()

    for copy in first_a + first_v + second_a + second_v + fourth + [swap]:
        copy.wait_send()
    sent = gn_ref.at[pl.ds(0, tall), pl.ds(0, 63 * wide)]
    pltpu.make_async_copy(sent, sent, a3_s).wait()
    pltpu.make_async_copy(v3.at[pl.ds(0, 15)], v3.at[pl.ds(0, 15)], v3_s).wait()


def store(gn_ref, gp_ref, gt_ref, gn_hbm, gp_hbm, gt_hbm, sem):
    width = gn_ref.shape[1] // STORES
    copies = [
        pltpu.make_async_copy(gn_ref.at[:, pl.ds(i * width, width)], gn_hbm.at[:, pl.ds(i * width, width)], sem.at[i])
        for i in range(STORES)
    ]
    copies.append(pltpu.make_async_copy(gp_ref, gp_hbm, sem.at[STORES]))
    copies.append(pltpu.make_async_copy(gt_ref, gt_hbm, sem.at[STORES + 1]))
    for copy in copies:
        copy.start()
    for copy in copies:
        copy.wait()


def body(counts, neuron_factors, pos_factors, trial_factors):
    k_dev, j_dev, i_dev = counts.shape
    ranks = neuron_factors.shape[0]
    vmem = pl.BlockSpec(memory_space=pltpu.VMEM)
    f32 = jnp.float32
    dma = pltpu.SemaphoreType.DMA
    gathered = pl.pallas_call(
        kernel,
        name="gradients",
        out_shape=(
            pltpu.VMEM((ranks, i_dev * lax.axis_size("neuron")), f32),
            pltpu.VMEM((ranks, j_dev * lax.axis_size("pos")), f32),
            pltpu.VMEM((ranks, k_dev * lax.axis_size("trial")), f32),
        ),
        in_specs=[pl.BlockSpec(memory_space=pltpu.HBM)] * 4,
        out_specs=(vmem, vmem, vmem),
        scratch_shapes=[
            pltpu.VMEM((ranks, i_dev), f32),
            pltpu.VMEM((ranks, j_dev), f32),
            pltpu.VMEM((ranks, k_dev), f32),
            pltpu.VMEM((k_dev, j_dev, i_dev), jnp.int32),
            pltpu.VMEM((LANES, LANES), f32),
            pltpu.VMEM((k_dev * j_dev, LANES), f32),
            pltpu.VMEM((ranks, i_dev), f32),
            pltpu.VMEM((ranks // 2, i_dev // 2), f32),
            pltpu.VMEM((2, 8, LANES), f32),
            pltpu.VMEM((8, LANES), f32),
            pltpu.VMEM((8, LANES), f32),
            pltpu.VMEM((5, 8, LANES), f32),
            pltpu.VMEM((3, ranks // 2, i_dev // 2), f32),
            pltpu.VMEM((3, ranks // 2, i_dev // 2), f32),
            pltpu.VMEM((7, 8, LANES), f32),
            pltpu.VMEM((3, 8, LANES), f32),
            pltpu.VMEM((16, 8, LANES), f32),
            pltpu.VMEM((5, 8, LANES), f32),
            dma((3,)), dma((LOADS,)),
            dma((3,)), dma((3,)), dma((3,)), dma((3,)),
            dma, dma((16,)), dma((16,)), dma((16,)),
            dma((7,)), dma((7,)), dma((3,)), dma((3,)),
            dma, dma((16,)), dma, dma,
            pltpu.SemaphoreType.REGULAR, pltpu.SemaphoreType.REGULAR, pltpu.SemaphoreType.REGULAR,
        ],
        compiler_params=pltpu.CompilerParams(
            collective_id=0, has_side_effects=True, vmem_limit_bytes=32 << 20
        ),
    )(*(pltpu.with_memory_space_constraint(one, pltpu.HBM) for one in (counts, neuron_factors, pos_factors, trial_factors)))
    return pl.pallas_call(
        store,
        name="store",
        out_shape=tuple(jax.ShapeDtypeStruct(one.shape, f32) for one in gathered),
        in_specs=[vmem] * 3,
        out_specs=(pl.BlockSpec(memory_space=pltpu.HBM),) * 3,
        scratch_shapes=[dma((STORES + 2,))],
    )(*(pltpu.with_memory_space_constraint(one, pltpu.VMEM) for one in gathered))


def solution(mesh):
    placed = (P("trial", "pos", "neuron"), P(None, "neuron"), P(None, "pos"), P(None, "trial"))
    return jax.shard_map(
        body, mesh=mesh, in_specs=placed, out_specs=(P(), P(), P()), check_vma=False
    )
```

```python
import jax
import jax.numpy as jnp
from jax import lax
from jax.experimental import pallas as pl
from jax.experimental.pallas import tpu as pltpu
from jax.sharding import PartitionSpec as P

MESH = pl.DeviceIdType.MESH
RING = (0, 1, -1, 2)
LANES = 128
ORDER_X = (3, 1, 2, 0)
ORDER_Y = (3, 1, 2, 0)
ORDER_Z = (0, 1, 3, 2)
VTURN = 3
VFIN = 15
LOADS = 8
HALF = 256
CHUNKS = 1
STORES = 4


def split(value):
    high = value.astype(jnp.bfloat16).astype(jnp.float32)
    return high, value - high


def kernel(
    counts_hbm, nf_hbm, pf_hbm, tf_hbm, gn_ref, gp_ref, gt_ref,
    nf_ref, pf_ref, tf_ref, counts, stage, proj, part_a, sum_a, part_v, sum_v, mean_v, final,
    a1, a2, v1, v2, v3, other,
    factor_sem, counts_sem, a1_s, a1_r, a2_s, a2_r, a3_s, a3_r, a4_s, a4_r, v1_s, v1_r, v2_s, v2_r, v3_s, v3_r, v4_s, v4_r,
    plane_sem, cube_sem, link_sem,
):
    ranks, i_dev = nf_ref.shape
    j_dev, k_dev = pf_ref.shape[1], tf_ref.shape[1]
    neurons = i_dev * lax.axis_size("neuron")
    positions = j_dev * lax.axis_size("pos")
    trials = k_dev * lax.axis_size("trial")
    chunks = CHUNKS
    k_chunk = k_dev // chunks
    rows = k_chunk * j_dev

    factors = []
    for at_sem, (src, dst) in enumerate(((pf_hbm, pf_ref), (tf_hbm, tf_ref), (nf_hbm, nf_ref))):
        load = pltpu.make_async_copy(src, dst, factor_sem.at[at_sem])
        load.start()
        factors.append(load)
    loads = []
    step = k_dev // LOADS
    for part in range(LOADS):
        load = pltpu.make_async_copy(
            counts_hbm.at[pl.ds(part * step, step)], counts.at[pl.ds(part * step, step)], counts_sem.at[part]
        )
        load.start()
        loads.append(load)

    me, y, z_hi = lax.axis_index("neuron"), lax.axis_index("pos"), lax.axis_index("trial")
    core, x, z_lo = lax.rem(me, 2), lax.rem(me // 2, 4), me // 8
    z = z_hi * 4 + z_lo
    sign = 1 - 2 * core
    steps_z = (0, 1, 2 * sign, -1)
    xs = [lax.rem(x + 4 + d, 4) for d in RING]
    xs_back = [lax.rem(x + 4 - d, 4) for d in RING]
    ys = [lax.rem(y + 4 + d, 4) for d in RING]
    ys_back = [lax.rem(y + 4 - d, 4) for d in RING]
    zs = [lax.rem(z + 16 + d, 16) for d in steps_z]
    zs_back = [lax.rem(z + 16 - d, 16) for d in steps_z]
    his = [lax.rem(z_hi + 4 + d, 4) for d in RING]
    his_back = [lax.rem(z_hi + 4 - d, 4) for d in RING]

    def at(x_, y_, z_, core_):
        return {"neuron": (lax.rem(z_, 4) * 4 + x_) * 2 + core_, "pos": y_, "trial": z_ // 4}

    def column(x_, z_):
        return (lax.rem(z_, 4) * 4 + x_) * 2 * i_dev

    barrier = pltpu.get_barrier_semaphore()
    greeted = [at(xs[a], y, z, 0) for a in (1, 2, 3)] + [at(x, ys[b], z, 0) for b in (1, 2, 3)]
    greeted += [at(x, y, lax.rem(z + 16 + d, 16), 1) for d in (8, 4, -4, 2, -2, 1, -1)]
    for device in greeted:
        pl.semaphore_signal(barrier, inc=1, device_id=device, device_id_type=MESH)

    def greet_core():
        pl.semaphore_signal(barrier, inc=1, device_id=at(x, y, z, 0), device_id_type=MESH)

    pl.when(core == 1)(greet_core)

    for load in factors:
        load.wait()
    nf, pf, tf = nf_ref[...], pf_ref[...], tf_ref[...]
    stage[...] = jnp.zeros_like(stage)
    for group in range(4):
        stage[pl.ds(group * ranks, ranks), pl.ds(0, j_dev)] = pf
        stage[pl.ds(group * ranks, ranks), pl.ds(j_dev, k_dev)] = tf
    turned = stage[...].T
    pf_t, tf_t = turned[:j_dev], turned[j_dev : j_dev + k_dev]
    lane = lax.broadcasted_iota(jnp.int32, (j_dev, LANES), 1)
    use_high = lax.rem(lane // ranks, 2) == 0
    nf_high, nf_low = split(nf)
    blank = jnp.zeros((LANES - 4 * ranks, i_dev), jnp.float32)
    nf_model = jnp.concatenate([nf_high, nf_high, nf_low, nf_low, blank], axis=0).astype(jnp.bfloat16)
    blank = jnp.zeros((LANES - 2 * ranks, i_dev), jnp.float32)
    nf_proj = jnp.concatenate([nf_high, nf_low, blank], axis=0).T.astype(jnp.bfloat16)
    pf_pair = jnp.concatenate([pf, pf], axis=1)
    left = lax.broadcasted_iota(jnp.int32, (ranks, LANES), 1) < j_dev

    half = HALF
    acc = [jnp.zeros((2 * ranks, half), jnp.float32) for _ in range(i_dev // half)]
    weights_t, weights = [], []
    for k in range(k_dev):
        high, low = split(pf_t * tf_t[k : k + 1])
        weights_t.append(jnp.where(use_high, high, low).astype(jnp.bfloat16))
    for k in range(0, k_dev, 2):
        high, low = split(pf_pair * jnp.where(left, tf[:, k : k + 1], tf[:, k + 1 : k + 2]))
        weights.append(jnp.concatenate([high, low], axis=0).astype(jnp.bfloat16))
    for chunk in range(chunks):
        k0 = chunk * k_chunk
        chunk_t = jnp.concatenate(weights_t[k0 : k0 + k_chunk], axis=0)
        chunk_w = jnp.concatenate(weights[k0 // 2 : (k0 + k_chunk) // 2], axis=1)
        models = [
            jnp.dot(chunk_t, nf_model[:, part * half : (part + 1) * half], preferred_element_type=jnp.float32)
            for part in range(i_dev // half)
        ]
        for load in loads[chunk * LOADS // chunks : (chunk + 1) * LOADS // chunks]:
            load.wait()
        projected = jnp.zeros((rows, LANES), jnp.float32)
        for part in range(i_dev // half):
            cols = slice(part * half, (part + 1) * half)
            model = models[part]
            guess = pl.reciprocal(model, approx=True)
            inverse = guess * (2.0 - model * guess)
            spikes = counts[k0 : k0 + k_chunk, :, cols].reshape(rows, half).astype(jnp.float32)
            ratio = 1.0 - spikes * inverse
            high = ratio.astype(jnp.bfloat16)
            low = (ratio - high.astype(jnp.float32)).astype(jnp.bfloat16)
            for piece in (high, low):
                acc[part] = acc[part] + jnp.dot(chunk_w, piece, preferred_element_type=jnp.float32)
                projected = projected + jnp.dot(piece, nf_proj[cols], preferred_element_type=jnp.float32)
        proj[pl.ds(k0 * j_dev, rows), :] = projected
    for part in range(i_dev // half):
        part_a[:, pl.ds(part * half, half)] = (acc[part][:ranks] + acc[part][ranks:]) / (positions * trials)

    def hear(count):
        pl.semaphore_wait(barrier, count)
        pl.semaphore_signal(link_sem, inc=1, device_id=at(x, y, z, 1 - core), device_id_type=MESH)

    def told():
        pl.semaphore_wait(link_sem, 1)

    pl.when(core == 0)(lambda: hear(13))
    pl.when(core == 1)(told)
    for a in (1, 2, 3):
        pl.semaphore_signal(plane_sem, inc=1, device_id=at(xs_back[a], y, z, core), device_id_type=MESH)

    def send(src, dst, send_sem, recv_sem, device):
        copy = pltpu.make_async_remote_copy(
            src_ref=src, dst_ref=dst, send_sem=send_sem, recv_sem=recv_sem, device_id=device, device_id_type=MESH
        )
        copy.start()
        return copy

    tall, wide = ranks // 2, i_dev // 2

    def quarter_of(ref, index, start):
        row, col = (index // 2) * tall, start + lax.rem(index, 2) * wide
        return ref.at[pl.ds(pl.multiple_of(row, tall), tall), pl.ds(pl.multiple_of(col, wide), wide)]

    first_a = [
        send(quarter_of(part_a, ys[d], 0), a1.at[d - 1], a1_s.at[d - 1], a1_r.at[d - 1], {"neuron": me, "pos": ys[d], "trial": z_hi})
        for d in (3, 1, 2)
    ]

    grad_b = jnp.zeros((j_dev, LANES), jnp.float32)
    grad_c = []
    for k in range(k_dev):
        block = proj[pl.ds(k * j_dev, j_dev), :]
        grad_b = grad_b + block * tf_t[k : k + 1]
        grad_c.append(jnp.sum(block * pf_t, axis=0, keepdims=True))
    stage[pl.ds(0, j_dev), :] = grad_b / (neurons * trials)
    stage[pl.ds(j_dev, LANES - j_dev), :] = jnp.zeros((LANES - j_dev, LANES), jnp.float32)
    stage[pl.ds(pl.multiple_of(j_dev + z_hi * k_dev, k_dev), k_dev), :] = jnp.concatenate(grad_c, axis=0) / (
        neurons * positions
    )
    turned = stage[...].T
    part_v[...] = (turned[:ranks] + turned[ranks : 2 * ranks]).reshape(part_v.shape)
    first_v = []
    for a in range(4):
        for c in range(2):
            if a or c:
                other_core = core if c == 0 else 1 - core
                slot = a * 2 + c - 1
                first_v.append(
                    send(part_v.at[other_core], v1.at[slot], v1_s.at[slot], v1_r.at[slot], at(xs[a], y, z, other_core))
                )

    for copy in first_a:
        copy.wait_recv()
    sum_a[...] = (a1[0] + a1[1]) + (a1[2] + quarter_of(part_a, y, 0)[...])
    pl.when(core == 1)(lambda: hear(14))
    pl.when(core == 0)(told)
    second_a = [
        send(sum_a, a2.at[h - 1], a2_s.at[h - 1], a2_r.at[h - 1], {"neuron": me, "pos": y, "trial": his[h]})
        for h in (3, 1, 2)
    ]
    pl.semaphore_wait(plane_sem, 3)
    for c in (1, 2, 3):
        pl.semaphore_signal(cube_sem, inc=1, device_id=at(x, y, zs_back[c], core), device_id_type=MESH)
    for copy in first_v:
        copy.wait_recv()
    total = part_v[core]
    for slot in range(7):
        total = total + v1[slot]
    sum_v[...] = total
    second_v = [
        send(sum_v, v2.at[h - 1], v2_s.at[h - 1], v2_r.at[h - 1], {"neuron": me, "pos": y, "trial": his[h]})
        for h in (3, 1, 2)
    ]

    for copy in second_a:
        copy.wait_recv()
    mine = quarter_of(gn_ref, y, me * i_dev)
    mine[...] = (a2[0] + a2[1]) + (a2[2] + sum_a[...])
    pl.semaphore_wait(cube_sem, 3)

    below = -1 - core
    lowest = lax.rem(z + below + 16, 16)
    first = jnp.where(lowest > 12, 16 - lowest, 0)
    for turn in range(4):
        dz = lax.rem(first + turn, 4) + below
        z_to, c = lax.rem(z + dz + 16, 16), lax.rem(dz + 4, 4)
        for x_to in (0, 1, 3, 2):
            dx = lax.rem(x_to - x + 4, 4)
            a = jnp.where(dx == 2, 3, jnp.where(dx == 3, 2, dx))
            for y_to in (0, 1, 3, 2):

                def give(a=a, c=c, x_to=x_to, y_to=y_to, z_to=z_to):
                    send(mine, mine, a3_s, a3_r.at[c * 4 + a], at(x_to, jnp.int32(y_to), z_to, core))

                pl.when((dz != 0) | (x != x_to) | (y != y_to))(give)
        if turn == VTURN:
            for copy in second_v:
                copy.wait_recv()
            mean_v[...] = (v2[0] + v2[1]) + (v2[2] + sum_v[...])
            v3[0] = mean_v[...]
        for late in range(turn + 1) if turn == VTURN else (turn,) if turn > VTURN else ():
            dz = lax.rem(first + late, 4) + below
            z_to, c = lax.rem(z + dz + 16, 16), lax.rem(dz + 4, 4)
            for b in ORDER_Y:

                def give_v(b=b, c=c, z_to=z_to):
                    slot = c * 4 + b
                    send(mean_v, v3.at[slot], v3_s, v3_r.at[slot], at(x, ys[b], z_to, core))

                if b:
                    give_v()
                else:
                    pl.when(dz != 0)(give_v)

    partner = {"neuron": me + sign, "pos": y, "trial": z_hi}

    def block_of(start):
        return gn_ref.at[:, pl.ds(pl.multiple_of(start, i_dev), i_dev)]

    def write(ref, row):
        for b in range(4):
            gp_ref[pl.ds(row, 8), pl.ds(b * j_dev, j_dev)] = ref[b][:, :j_dev]
        gt_ref[pl.ds(row, 8), :] = ref[4][:, j_dev:]

    fourth = []
    for turn, (a, c) in enumerate((a, c) for a in ORDER_X for c in ORDER_Z):
        if turn == VFIN:
            for slot in range(1, 16):
                pltpu.make_async_copy(v3.at[slot], v3.at[slot], v3_r.at[slot]).wait()
            all_c = jnp.zeros((8, LANES), jnp.float32)
            for b in range(4):
                over_z = (v3[b] + v3[4 + b]) + (v3[8 + b] + v3[12 + b])
                all_c = all_c + over_z
                final[ys_back[b]] = over_z
            final[4] = all_c
            swap = send(final, other, v4_s, v4_r, partner)
            write(final, pl.multiple_of(core * 8, 8))
        slot = c * 4 + a
        block = block_of(column(xs_back[a], zs_back[c]) + core * i_dev)
        if slot == 0:
            landed = gn_ref.at[pl.ds(0, tall), pl.ds(0, 3 * wide)]
        else:
            landed = block
        pltpu.make_async_copy(landed, landed, a3_r.at[slot]).wait()
        fourth.append(send(block, block, a4_s.at[slot], a4_r.at[slot], partner))
    swap.wait_recv()
    write(other, pl.multiple_of((1 - core) * 8, 8))
    for copy in fourth:
        copy.wait_recv()

    for copy in first_a + first_v + second_a + second_v + fourth + [swap]:
        copy.wait_send()
    sent = gn_ref.at[pl.ds(0, tall), pl.ds(0, 63 * wide)]
    pltpu.make_async_copy(sent, sent, a3_s).wait()
    pltpu.make_async_copy(v3.at[pl.ds(0, 15)], v3.at[pl.ds(0, 15)], v3_s).wait()


def store(gn_ref, gp_ref, gt_ref, gn_hbm, gp_hbm, gt_hbm, sem):
    width = gn_ref.shape[1] // STORES
    copies = [
        pltpu.make_async_copy(gn_ref.at[:, pl.ds(i * width, width)], gn_hbm.at[:, pl.ds(i * width, width)], sem.at[i])
        for i in range(STORES)
    ]
    copies.append(pltpu.make_async_copy(gp_ref, gp_hbm, sem.at[STORES]))
    copies.append(pltpu.make_async_copy(gt_ref, gt_hbm, sem.at[STORES + 1]))
    for copy in copies:
        copy.start()
    for copy in copies:
        copy.wait()


def body(counts, neuron_factors, pos_factors, trial_factors):
    k_dev, j_dev, i_dev = counts.shape
    ranks = neuron_factors.shape[0]
    vmem = pl.BlockSpec(memory_space=pltpu.VMEM)
    f32 = jnp.float32
    dma = pltpu.SemaphoreType.DMA
    gathered = pl.pallas_call(
        kernel,
        name="gradients",
        out_shape=(
            pltpu.VMEM((ranks, i_dev * lax.axis_size("neuron")), f32),
            pltpu.VMEM((ranks, j_dev * lax.axis_size("pos")), f32),
            pltpu.VMEM((ranks, k_dev * lax.axis_size("trial")), f32),
        ),
        in_specs=[pl.BlockSpec(memory_space=pltpu.HBM)] * 4,
        out_specs=(vmem, vmem, vmem),
        scratch_shapes=[
            pltpu.VMEM((ranks, i_dev), f32),
            pltpu.VMEM((ranks, j_dev), f32),
            pltpu.VMEM((ranks, k_dev), f32),
            pltpu.VMEM((k_dev, j_dev, i_dev), jnp.int32),
            pltpu.VMEM((LANES, LANES), f32),
            pltpu.VMEM((k_dev * j_dev, LANES), f32),
            pltpu.VMEM((ranks, i_dev), f32),
            pltpu.VMEM((ranks // 2, i_dev // 2), f32),
            pltpu.VMEM((2, 8, LANES), f32),
            pltpu.VMEM((8, LANES), f32),
            pltpu.VMEM((8, LANES), f32),
            pltpu.VMEM((5, 8, LANES), f32),
            pltpu.VMEM((3, ranks // 2, i_dev // 2), f32),
            pltpu.VMEM((3, ranks // 2, i_dev // 2), f32),
            pltpu.VMEM((7, 8, LANES), f32),
            pltpu.VMEM((3, 8, LANES), f32),
            pltpu.VMEM((16, 8, LANES), f32),
            pltpu.VMEM((5, 8, LANES), f32),
            dma((3,)), dma((LOADS,)),
            dma((3,)), dma((3,)), dma((3,)), dma((3,)),
            dma, dma((16,)), dma((16,)), dma((16,)),
            dma((7,)), dma((7,)), dma((3,)), dma((3,)),
            dma, dma((16,)), dma, dma,
            pltpu.SemaphoreType.REGULAR, pltpu.SemaphoreType.REGULAR, pltpu.SemaphoreType.REGULAR,
        ],
        compiler_params=pltpu.CompilerParams(
            collective_id=0, has_side_effects=True, vmem_limit_bytes=32 << 20
        ),
    )(*(pltpu.with_memory_space_constraint(one, pltpu.HBM) for one in (counts, neuron_factors, pos_factors, trial_factors)))
    return pl.pallas_call(
        store,
        name="store",
        out_shape=tuple(jax.ShapeDtypeStruct(one.shape, f32) for one in gathered),
        in_specs=[vmem] * 3,
        out_specs=(pl.BlockSpec(memory_space=pltpu.HBM),) * 3,
        scratch_shapes=[dma((STORES + 2,))],
    )(*(pltpu.with_memory_space_constraint(one, pltpu.VMEM) for one in gathered))


def solution(mesh):
    placed = (P("trial", "pos", "neuron"), P(None, "neuron"), P(None, "pos"), P(None, "trial"))
    return jax.shard_map(
        body, mesh=mesh, in_specs=placed, out_specs=(P(), P(), P()), check_vma=False
    )
```
